32 devices in a mesh: grp: 2 (over y), pipe: 8 (over z, x), head: 2 (over core).
Axes of the slice: x: 2, y: 2, z: 4, core: 2. Of those that a mesh axis runs over, the one named last changes fastest.
Arguments:
- queries: bfloat16 [512, 64, 128], P(('grp', 'pipe'), 'head'), parts along dimension 0, may hold values from -10 to 10
- slice_own_keys: bfloat16 [512, 4, 128], P(('grp', 'pipe'), 'head'), parts along dimension 0, may hold values from -6 to 6
- slice_own_values: bfloat16 [512, 4, 128], P(('grp', 'pipe'), 'head'), parts along dimension 0, may hold values from -6 to 6
- cache_keys: bfloat16 [1664, 4, 128], P(('grp', 'pipe'), 'head'), parts along dimension 0, may hold values from -8 to 8
- context_value_rows: bfloat16 [1664, 4, 128], P(('grp', 'pipe'), 'head'), parts along dimension 0, may hold values from -6 to 6
- prefix_len: int32 [16], P('grp'), parts along dimension 0, may hold values from 1 to 832, as said below
Outputs:
- advanced: bfloat16 [512, 64, 128], P(('grp', 'pipe'), 'head'), parts along dimension 0
The draws below stay inside these ranges and needn't reach their ends.
There are 2 independent parts, one for each index of `grp`. The reference program is written for one: setup_inputs(seed, part) draws one part's arguments, and reference() takes and returns one part's arrays. A program takes and returns all parts, laid end to end along the dimension named above; each array names one. Nothing has to cross between parts.
Inputs may be any that keep to these rules, and one draw needn't show every extreme that they name: prefix_len[p] lies in ((8 - 1 - p) * 104, (8 - p) * 104]; prefix_len[0] is 832 and the last section's is 1.
All inputs are finite; a program needn't handle non-finite values.
Results may differ from the reference program's by a relative error of at most 0.012.
Values may be sent and summed in bfloat16 or wider, within the bound.
A program may use at most 64 MiB of HBM per device.

```python
import math
import jax
import jax.numpy as jnp
from jax import lax

HQ = 64
KEY_VALUE_HEADS = 4
HEAD_DIMENSION = 128
SLICE = 32
BLK = 104
QUERY_TOKENS = 256
CONTEXT_SPAN = 832


def draw_queries(key, part):
    complete_shape = (QUERY_TOKENS, HQ, HEAD_DIMENSION)
    scale_factors = jnp.exp(jax.random.uniform(jax.random.fold_in(key, 12), (QUERY_TOKENS, HQ, 1), jnp.float32, math.log(0.2), math.log(2.0)))
    noise_draw = jax.random.normal(jax.random.fold_in(key, 11), complete_shape, jnp.float32)
    drawn = jnp.clip(noise_draw * scale_factors, -10.0, 10.0)
    return drawn.astype(jnp.bfloat16)


def draw_cache_keys(key, part):
    complete_shape = (CONTEXT_SPAN, KEY_VALUE_HEADS, HEAD_DIMENSION)
    scale_factors = jnp.exp(jax.random.uniform(jax.random.fold_in(key, 14), (CONTEXT_SPAN, KEY_VALUE_HEADS, 1), jnp.float32, math.log(0.35), math.log(3.5)))
    noise_draw = jax.random.normal(jax.random.fold_in(key, 13), complete_shape, jnp.float32)
    drawn = jnp.clip(noise_draw * scale_factors, -8.0, 8.0)
    return drawn.astype(jnp.bfloat16)


def draw_prefix_len(key, part):
    sections = CONTEXT_SPAN // BLK
    section_index = jnp.arange(sections)
    jitter = jax.random.randint(jax.random.fold_in(key, 21), (sections,), 1, BLK + 1)
    jitter = jnp.where(section_index == 0, BLK, jnp.where(section_index == sections - 1, 1, jitter))
    return ((sections - 1 - section_index) * BLK + jitter).astype(jnp.int32)


def steps_of(own_key, shape, split, smallest, top_value):
    factor_of, own = 1.0, jax.random.fold_in(own_key, 6)
    for dim, blocks in split:
        draws = jnp.exp(jax.random.uniform(jax.random.fold_in(own, dim), (blocks,), jnp.float32, smallest / len(split), top_value / len(split)))
        factor_of = factor_of * jnp.repeat(draws, shape[dim] // blocks).reshape([-1 if axis == dim else 1 for axis in range(len(shape))])
    return factor_of


def scatter_about(own_key, dims, width, most, cuts=(), held_as=jnp.bfloat16):
    result = width * jax.random.normal(own_key, dims, jnp.float32)
    if cuts:
        result = result * steps_of(own_key, dims, cuts, -0.22, 0.18)
    return jnp.clip(result, -most, most).astype(held_as)


def setup_inputs(seed: int = 0, part: int = 0) -> dict:
    key_of = jax.random.split(jax.random.key(seed), 7)
    part_keys = jax.random.split(jax.random.fold_in(key_of[6], part), 7)
    return {
        "queries": draw_queries(jax.random.fold_in(jax.random.fold_in(key_of[6], part), 71), part),
        "slice_own_keys": scatter_about(part_keys[1], (QUERY_TOKENS, KEY_VALUE_HEADS, HEAD_DIMENSION), 1.0, 6.0, ((0, 8), (1, 2))),
        "slice_own_values": scatter_about(part_keys[2], (QUERY_TOKENS, KEY_VALUE_HEADS, HEAD_DIMENSION), 1.0, 6.0, ((0, 8), (1, 2))),
        "cache_keys": draw_cache_keys(jax.random.fold_in(jax.random.fold_in(key_of[6], part), 71), part),
        "context_value_rows": scatter_about(part_keys[4], (CONTEXT_SPAN, KEY_VALUE_HEADS, HEAD_DIMENSION), 1.0, 6.0, ((0, 8), (1, 2))),
        "prefix_len": draw_prefix_len(jax.random.fold_in(jax.random.fold_in(key_of[6], part), 71), part),
    }


def reference(queries, slice_own_keys, slice_own_values, cache_keys, context_value_rows, prefix_len):
    token_count, head_count, head_width = queries.shape
    groups = slice_own_keys.shape[1]
    per_group = head_count // groups
    sections = token_count // SLICE
    context = cache_keys.shape[0]
    factor = 1.0 / math.sqrt(head_width)
    cached_keys = cache_keys.astype(jnp.float32)
    cached_values = context_value_rows.astype(jnp.float32)

    def section_output(pieces):
        query_block, key_block, value_block, prefix = pieces
        all_keys = jnp.concatenate([cached_keys, key_block.astype(jnp.float32)], axis=0)
        all_values = jnp.concatenate([cached_values, value_block.astype(jnp.float32)], axis=0)
        scores = jnp.einsum('sghd,kgd->gkhs', query_block.astype(jnp.float32), all_keys) * factor
        key_index = lax.broadcasted_iota(jnp.int32, (1, context + SLICE, 1, SLICE), 1)
        row_index = lax.broadcasted_iota(jnp.int32, (1, context + SLICE, 1, SLICE), 3)
        visible = jnp.where(key_index < context, key_index < prefix, key_index - context <= row_index)
        row_max = lax.optimization_barrier(jnp.max(jnp.where(visible, scores, -1e+30), axis=1))
        weights = jnp.where(visible, jnp.exp(scores - row_max[:, None]), 0.0)
        row_sum = lax.optimization_barrier(jnp.sum(weights, axis=1))
        rounded = lax.optimization_barrier(weights.astype(jnp.bfloat16)).astype(jnp.float32)
        weighted = jnp.einsum('gkhs,kgd->sghd', rounded, all_values)
        attended = weighted / jnp.transpose(row_sum, (2, 0, 1))[..., None]
        return attended.astype(jnp.bfloat16).reshape(SLICE, head_count, head_width)
    outputs = lax.map(section_output, (queries.reshape(sections, SLICE, groups, per_group, head_width), slice_own_keys.reshape(sections, SLICE, groups, head_width), slice_own_values.reshape(sections, SLICE, groups, head_width), prefix_len))
    return jnp.roll(outputs, 1, axis=0).reshape(token_count, head_count, head_width)
```

```python
import functools
import math

import jax
import jax.numpy as jnp
from jax import lax
from jax.experimental import pallas as pl
from jax.experimental.pallas import tpu as pltpu
from jax.sharding import PartitionSpec as P

MESH = pl.DeviceIdType.MESH


def attend_kernel(
    n,
    prefix_ref,
    q_ref,
    own_k_ref,
    own_v_ref,
    key_ref,
    value_ref,
    out_ref,
    kv,
    acc,
    top,
    total,
    stage,
    send_sem,
    recv_sem,
    out_send,
    out_recv,
):
    rows_r = n // 2
    slice_rows, heads, width = q_ref.shape
    groups = kv.shape[1]
    per_group = heads // groups
    columns = slice_rows * per_group
    block = kv.shape[2]
    scale = math.log2(math.e) / math.sqrt(width)
    me = lax.axis_index("pipe")
    z, c = me // 2, me % 2

    barrier = pltpu.get_barrier_semaphore()
    for step in (1, 2, n - 2, n - 1):
        pl.semaphore_signal(
            barrier, inc=1, device_id={"pipe": (me + step) % n}, device_id_type=MESH
        )

    def pick(raw_ref, g):
        count = raw_ref.shape[0] // groups
        row = lax.broadcasted_iota(jnp.int32, (count, count * groups), 0)
        col = lax.broadcasted_iota(jnp.int32, (count, count * groups), 1)
        chosen = jnp.where(col == row * groups + g, 1.0, 0.0).astype(jnp.bfloat16)
        return jnp.dot(chosen, raw_ref[...], preferred_element_type=jnp.float32).astype(
            jnp.bfloat16
        )

    for g in range(groups):
        kv[me, g, :, :width] = pick(key_ref, g)
        kv[me, g, :, width:] = pick(value_ref, g)
    pl.semaphore_wait(barrier, 4)

    def copy(direction, b, g, target):
        return pltpu.make_async_remote_copy(
            src_ref=kv.at[b, g],
            dst_ref=kv.at[b, g],
            send_sem=send_sem.at[direction, b, g],
            recv_sem=recv_sem.at[b, g],
            device_id={"pipe": target},
            device_id_type=MESH,
        )

    def down_if(zb):
        return (zb >= z) & (zb < rows_r) & (z > 0)

    def up_if(zb):
        return (zb >= 0) & (zb <= z) & (z + 1 <= rows_r - 1 - zb)

    def across_if(zb):
        return (zb >= 0) & (zb < rows_r) & (z <= rows_r - 1 - zb)

    def sends(zb, act, downward, upward):
        b = zb * 2 + c
        for g in range(groups):
            if downward:

                @pl.when(down_if(zb))
                def _():
                    act(copy(0, b, g, me - 2))

            if upward:

                @pl.when(up_if(zb))
                def _():
                    act(copy(1, b, g, me + 2))

            @pl.when(across_if(zb))
            def _():
                act(copy(2, b, g, z * 2 + 1 - c))

    sends(z, lambda dma: dma.start(), True, True)

    def query(g):
        return q_ref[:, g * per_group : (g + 1) * per_group, :].reshape(columns, width)

    def scores(keys, g):
        return lax.dot_general(
            keys, query(g), (((1,), (1,)), ((), ())), preferred_element_type=jnp.float32
        )

    def gather(values, weights):
        return lax.dot_general(
            values,
            weights.astype(jnp.bfloat16),
            (((0,), (0,)), ((), ())),
            preferred_element_type=jnp.float32,
        )

    for g in range(groups):
        s = scores(pick(own_k_ref, g), g)
        key_index = lax.broadcasted_iota(jnp.int32, s.shape, 0)
        row_index = lax.broadcasted_iota(jnp.int32, s.shape, 1) // per_group
        s = jnp.where(key_index <= row_index, s, -1e30)
        m = jnp.max(s, axis=0, keepdims=True)
        w = jnp.exp2((s - m) * scale)
        top[g] = m
        total[g] = jnp.sum(w, axis=0, keepdims=True)
        acc[g] = gather(pick(own_v_ref, g), w)

    prefix = prefix_ref[me]

    def absorb(b, g):
        s = scores(kv[b, g, :, :width], g)
        key_index = lax.broadcasted_iota(jnp.int32, s.shape, 0)
        s = jnp.where(key_index < prefix - b * block, s, -1e30)
        old = top[g]
        m = jnp.maximum(old, jnp.max(s, axis=0, keepdims=True))
        w = jnp.exp2((s - m) * scale)
        fade = jnp.exp2((old - m) * scale)
        top[g] = m
        total[g] = total[g] * fade + jnp.sum(w, axis=0, keepdims=True)
        acc[g] = acc[g] * fade + gather(kv[b, g, :, width:], w)

    def wait_recv(b, g):
        copy(0, b, g, me).wait_recv()

    def from_above(d):
        return (d > 0) & (z + d < rows_r)

    def from_below(d):
        return (d > 0) & (z - d >= 0) & (z <= rows_r - 1 - (z - d))

    def step(d, carry):
        @pl.when(from_above(d))
        def _():
            for g in range(groups):
                wait_recv((z + d) * 2 + c, g)
            sends(z + d, lambda dma: dma.start(), True, False)

        @pl.when(from_below(d))
        def _():
            for g in range(groups):
                wait_recv((z - d) * 2 + c, g)
            sends(z - d, lambda dma: dma.start(), False, True)

        def use(j, inner):
            crossing = j // 2
            sign = 1 - 2 * (j % 2)
            reach = d - crossing
            zb = z + sign * reach
            b = zb * 2 + jnp.where(crossing == 1, 1 - c, c)
            there = (reach >= 0) & (zb >= 0) & (zb < rows_r) & ((reach > 0) | (sign > 0))
            needed = there & (b <= n - 1 - me)

            @pl.when(needed)
            def _():
                @pl.when(crossing == 1)
                def _():
                    for g in range(groups):
                        wait_recv(b, g)

                for g in range(groups):
                    absorb(b, g)

            return inner

        lax.fori_loop(0, 4, use, 0)
        return carry

    lax.fori_loop(0, rows_r + 1, step, 0)

    outs = []
    for g in range(groups):
        done = jnp.transpose(acc[g] / total[g])
        part = pl.ds(g * per_group, per_group)
        stage[:, part, :] = done.astype(jnp.bfloat16).reshape(slice_rows, per_group, width)
        dma = pltpu.make_async_remote_copy(
            src_ref=stage.at[:, part, :],
            dst_ref=out_ref.at[:, part, :],
            send_sem=out_send.at[g],
            recv_sem=out_recv.at[g],
            device_id={"pipe": (me + 1) % n},
            device_id_type=MESH,
        )
        dma.start()
        outs.append(dma)

    def drain(d, carry):
        @pl.when(from_above(d))
        def _():
            sends(z + d, lambda dma: dma.wait_send(), True, False)

        @pl.when(from_below(d))
        def _():
            sends(z - d, lambda dma: dma.wait_send(), False, True)

        return carry

    sends(z, lambda dma: dma.wait_send(), True, True)
    lax.fori_loop(1, rows_r, drain, 0)
    for dma in outs:
        dma.wait()


def fused(queries, slice_own_keys, slice_own_values, cache_keys, context_value_rows, prefix_len):
    n = lax.axis_size("pipe")
    slice_rows, heads, width = queries.shape
    block, groups, _ = cache_keys.shape
    columns = slice_rows * heads // groups
    vmem = pl.BlockSpec(memory_space=pltpu.VMEM)
    return pl.pallas_call(
        functools.partial(attend_kernel, n),
        out_shape=jax.ShapeDtypeStruct(queries.shape, jnp.bfloat16),
        in_specs=[pl.BlockSpec(memory_space=pltpu.SMEM)] + [vmem] * 5,
        out_specs=vmem,
        scratch_shapes=[
            pltpu.VMEM((n, groups, block, 2 * width), jnp.bfloat16),
            pltpu.VMEM((groups, width, columns), jnp.float32),
            pltpu.VMEM((groups, 1, columns), jnp.float32),
            pltpu.VMEM((groups, 1, columns), jnp.float32),
            pltpu.VMEM(queries.shape, jnp.bfloat16),
            pltpu.SemaphoreType.DMA((3, n, groups)),
            pltpu.SemaphoreType.DMA((n, groups)),
            pltpu.SemaphoreType.DMA((groups,)),
            pltpu.SemaphoreType.DMA((groups,)),
        ],
        compiler_params=pltpu.CompilerParams(
            collective_id=0, has_side_effects=True, vmem_limit_bytes=40 * 1024 * 1024
        ),
        name="relay_attention",
    )(
        prefix_len,
        queries,
        slice_own_keys.reshape(-1, width),
        slice_own_values.reshape(-1, width),
        cache_keys.reshape(-1, width),
        context_value_rows.reshape(-1, width),
    )


def solution(mesh):
    in_specs = (
        P(("grp", "pipe"), "head", None),
        P(("grp", "pipe"), "head", None),
        P(("grp", "pipe"), "head", None),
        P(("grp", "pipe"), "head", None),
        P(("grp", "pipe"), "head", None),
        P("grp"),
    )
    out_specs = P(("grp", "pipe"), "head", None)
    return jax.shard_map(fused, mesh=mesh, in_specs=in_specs, out_specs=out_specs, check_vma=False)
```

```python
import functools
import math

import jax
import jax.numpy as jnp
from jax import lax
from jax.experimental import pallas as pl
from jax.experimental.pallas import tpu as pltpu
from jax.sharding import PartitionSpec as P

MESH = pl.DeviceIdType.MESH


def attend_kernel(
    n,
    prefix_hbm,
    q_hbm,
    own_k_hbm,
    own_v_hbm,
    key_hbm,
    value_hbm,
    out_ref,
    prefix_ref,
    q_ref,
    own_k_ref,
    own_v_ref,
    key_ref,
    value_ref,
    load_sem,
    kv,
    turned,
    acc,
    top,
    total,
    stage,
    send_sem,
    recv_sem,
    out_send,
    out_recv,
):
    rows_r = n // 2
    slice_rows, heads, width = q_ref.shape
    groups = kv.shape[1]
    per_group = heads // groups
    columns = slice_rows * per_group
    block = kv.shape[2]
    scale = math.log2(math.e) / math.sqrt(width)
    me = lax.axis_index("pipe")
    z, c = me // 2, me % 2

    loads = [
        pltpu.make_async_copy(source, target, load_sem.at[i])
        for i, (source, target) in enumerate(
            (
                (key_hbm, key_ref),
                (value_hbm, value_ref),
                (own_k_hbm, own_k_ref),
                (own_v_hbm, own_v_ref),
                (q_hbm, q_ref),
                (prefix_hbm, prefix_ref),
            )
        )
    ]
    for load in loads:
        load.start()
    barrier = pltpu.get_barrier_semaphore()
    for step in (1, 2, n - 2, n - 1):
        pl.semaphore_signal(
            barrier, inc=1, device_id={"pipe": (me + step) % n}, device_id_type=MESH
        )

    def pick(raw_ref, g):
        count = raw_ref.shape[0] // groups
        row = lax.broadcasted_iota(jnp.int32, (count, count * groups), 0)
        col = lax.broadcasted_iota(jnp.int32, (count, count * groups), 1)
        chosen = jnp.where(col == row * groups + g, 1.0, 0.0).astype(jnp.bfloat16)
        return jnp.dot(chosen, raw_ref[...], preferred_element_type=jnp.float32).astype(
            jnp.bfloat16
        )

    loads[0].wait()
    loads[1].wait()
    for g in range(groups):
        kv[me, g, :, :width] = pick(key_ref, g)
        kv[me, g, :, width:] = pick(value_ref, g)
    pl.semaphore_wait(barrier, 4)

    def copy(direction, b, g, target):
        return pltpu.make_async_remote_copy(
            src_ref=kv.at[b, g],
            dst_ref=kv.at[b, g],
            send_sem=send_sem.at[direction, b, g],
            recv_sem=recv_sem.at[b, g],
            device_id={"pipe": target},
            device_id_type=MESH,
        )

    def down_if(zb):
        return (zb >= z) & (zb < rows_r) & (z > 0)

    def up_if(zb):
        return (zb >= 0) & (zb <= z) & (z + 1 <= rows_r - 1 - zb)

    def across_if(zb):
        return (zb >= 0) & (zb < rows_r) & (z <= rows_r - 1 - zb)

    def sends(zb, g, act, downward, upward):
        b = zb * 2 + c
        if downward:

            @pl.when(down_if(zb))
            def _():
                act(copy(0, b, g, me - 2))

        if upward:

            @pl.when(up_if(zb))
            def _():
                act(copy(1, b, g, me + 2))

        @pl.when(across_if(zb))
        def _():
            act(copy(2, b, g, z * 2 + 1 - c))

    for g in range(groups):
        sends(z, g, lambda dma: dma.start(), True, True)

    for load in loads[2:]:
        load.wait()

    def query(g):
        return q_ref[:, g * per_group : (g + 1) * per_group, :].reshape(columns, width)

    for g in range(groups):
        turned[g] = jnp.transpose(query(g))

    def scores(keys, g):
        return jnp.dot(keys, turned[g], preferred_element_type=jnp.float32)

    def gather(values, weights):
        return lax.dot_general(
            values,
            weights.astype(jnp.bfloat16),
            (((0,), (0,)), ((), ())),
            preferred_element_type=jnp.float32,
        )

    for g in range(groups):
        s = scores(pick(own_k_ref, g), g)
        key_index = lax.broadcasted_iota(jnp.int32, s.shape, 0)
        row_index = lax.broadcasted_iota(jnp.int32, s.shape, 1) // per_group
        s = jnp.where(key_index <= row_index, s, -1e30)
        m = jnp.max(s, axis=0, keepdims=True)
        w = jnp.exp2((s - m) * scale)
        top[g] = m
        total[g] = jnp.sum(w, axis=0, keepdims=True)
        acc[g] = gather(pick(own_v_ref, g), w)

    prefix = prefix_ref[me]

    def absorb(b, g):
        s = scores(kv[b, g, :, :width], g)
        key_index = lax.broadcasted_iota(jnp.int32, s.shape, 0)
        s = jnp.where(key_index < prefix - b * block, s, -1e30)
        old = top[g]
        m = jnp.maximum(old, jnp.max(s, axis=0, keepdims=True))
        w = jnp.exp2((s - m) * scale)
        fade = jnp.exp2((old - m) * scale)
        top[g] = m
        total[g] = total[g] * fade + jnp.sum(w, axis=0, keepdims=True)
        acc[g] = acc[g] * fade + gather(kv[b, g, :, width:], w)

    def wait_recv(b, g):
        copy(0, b, g, me).wait_recv()

    def from_above(d):
        return (d > 0) & (z + d < rows_r)

    def from_below(d):
        return (d > 0) & (z - d >= 0) & (z <= rows_r - 1 - (z - d))

    def step(d, carry):
        for g in range(groups):

            @pl.when(from_above(d))
            def _():
                wait_recv((z + d) * 2 + c, g)
                sends(z + d, g, lambda dma: dma.start(), True, False)

            @pl.when(from_below(d))
            def _():
                wait_recv((z - d) * 2 + c, g)
                sends(z - d, g, lambda dma: dma.start(), False, True)

        def use(j, inner):
            crossing = j // 2
            sign = 1 - 2 * (j % 2)
            reach = d - crossing
            zb = z + sign * reach
            b = zb * 2 + jnp.where(crossing == 1, 1 - c, c)
            there = (reach >= 0) & (zb >= 0) & (zb < rows_r) & ((reach > 0) | (sign > 0))
            needed = there & (b <= n - 1 - me)

            @pl.when(needed)
            def _():
                @pl.when(crossing == 1)
                def _():
                    for g in range(groups):
                        wait_recv(b, g)

                for g in range(groups):
                    absorb(b, g)

            return inner

        lax.fori_loop(0, 4, use, 0)
        return carry

    lax.fori_loop(0, rows_r + 1, step, 0)

    outs = []
    for g in range(groups):
        done = jnp.transpose(acc[g] / total[g])
        part = pl.ds(g * per_group, per_group)
        stage[:, part, :] = done.astype(jnp.bfloat16).reshape(slice_rows, per_group, width)
        dma = pltpu.make_async_remote_copy(
            src_ref=stage.at[:, part, :],
            dst_ref=out_ref.at[:, part, :],
            send_sem=out_send.at[g],
            recv_sem=out_recv.at[g],
            device_id={"pipe": (me + 1) % n},
            device_id_type=MESH,
        )
        dma.start()
        outs.append(dma)

    def drain(d, carry):
        for g in range(groups):

            @pl.when(from_above(d))
            def _():
                sends(z + d, g, lambda dma: dma.wait_send(), True, False)

            @pl.when(from_below(d))
            def _():
                sends(z - d, g, lambda dma: dma.wait_send(), False, True)

        return carry

    for g in range(groups):
        sends(z, g, lambda dma: dma.wait_send(), True, True)
    lax.fori_loop(1, rows_r, drain, 0)
    for dma in outs:
        dma.wait()


def fused(queries, slice_own_keys, slice_own_values, cache_keys, context_value_rows, prefix_len):
    n = lax.axis_size("pipe")
    slice_rows, heads, width = queries.shape
    block, groups, _ = cache_keys.shape
    columns = slice_rows * heads // groups
    return pl.pallas_call(
        functools.partial(attend_kernel, n),
        out_shape=jax.ShapeDtypeStruct(queries.shape, jnp.bfloat16),
        in_specs=[pl.BlockSpec(memory_space=pltpu.HBM)] * 6,
        out_specs=pl.BlockSpec(memory_space=pltpu.VMEM),
        scratch_shapes=[
            pltpu.SMEM(prefix_len.shape, jnp.int32),
            pltpu.VMEM(queries.shape, jnp.bfloat16),
            pltpu.VMEM((slice_rows * groups, width), jnp.bfloat16),
            pltpu.VMEM((slice_rows * groups, width), jnp.bfloat16),
            pltpu.VMEM((block * groups, width), jnp.bfloat16),
            pltpu.VMEM((block * groups, width), jnp.bfloat16),
            pltpu.SemaphoreType.DMA((6,)),
            pltpu.VMEM((n, groups, block, 2 * width), jnp.bfloat16),
            pltpu.VMEM((groups, width, columns), jnp.bfloat16),
            pltpu.VMEM((groups, width, columns), jnp.float32),
            pltpu.VMEM((groups, 1, columns), jnp.float32),
            pltpu.VMEM((groups, 1, columns), jnp.float32),
            pltpu.VMEM(queries.shape, jnp.bfloat16),
            pltpu.SemaphoreType.DMA((3, n, groups)),
            pltpu.SemaphoreType.DMA((n, groups)),
            pltpu.SemaphoreType.DMA((groups,)),
            pltpu.SemaphoreType.DMA((groups,)),
        ],
        compiler_params=pltpu.CompilerParams(
            collective_id=0, has_side_effects=True, vmem_limit_bytes=63 * 1024 * 1024
        ),
        name="relay_attention",
    )(
        prefix_len,
        queries,
        slice_own_keys.reshape(-1, width),
        slice_own_values.reshape(-1, width),
        cache_keys.reshape(-1, width),
        context_value_rows.reshape(-1, width),
    )


def solution(mesh):
    in_specs = (
        P(("grp", "pipe"), "head", None),
        P(("grp", "pipe"), "head", None),
        P(("grp", "pipe"), "head", None),
        P(("grp", "pipe"), "head", None),
        P(("grp", "pipe"), "head", None),
        P("grp"),
    )
    out_specs = P(("grp", "pipe"), "head", None)
    return jax.shard_map(fused, mesh=mesh, in_specs=in_specs, out_specs=out_specs, check_vma=False)
```

```python
import functools
import math

import jax
import jax.numpy as jnp
from jax import lax
from jax.experimental import pallas as pl
from jax.experimental.pallas import tpu as pltpu
from jax.sharding import PartitionSpec as P

MESH = pl.DeviceIdType.MESH


def attend_kernel(
    n,
    prefix_hbm,
    q_hbm,
    own_k_hbm,
    own_v_hbm,
    key_hbm,
    value_hbm,
    out_ref,
    prefix_ref,
    q_ref,
    own_k_ref,
    own_v_ref,
    key_ref,
    value_ref,
    load_sem,
    kv,
    turned,
    acc,
    top,
    total,
    stage,
    send_sem,
    recv_sem,
    out_send,
    out_recv,
):
    rows_r = n // 2
    slice_rows, heads, width = q_ref.shape
    groups = kv.shape[1]
    per_group = heads // groups
    columns = slice_rows * per_group
    block = kv.shape[2]
    scale = math.log2(math.e) / math.sqrt(width)
    me = lax.axis_index("pipe")
    z, c = me // 2, me % 2

    loads = [
        pltpu.make_async_copy(source, target, load_sem.at[i])
        for i, (source, target) in enumerate(
            (
                (key_hbm, key_ref),
                (value_hbm, value_ref),
                (own_k_hbm, own_k_ref),
                (own_v_hbm, own_v_ref),
                (q_hbm, q_ref),
                (prefix_hbm, prefix_ref),
            )
        )
    ]
    for load in loads:
        load.start()
    barrier = pltpu.get_barrier_semaphore()
    for step in (1, 2, n - 2, n - 1):
        pl.semaphore_signal(
            barrier, inc=1, device_id={"pipe": (me + step) % n}, device_id_type=MESH
        )

    def pick(raw_ref, g):
        count = raw_ref.shape[0] // groups
        row = lax.broadcasted_iota(jnp.int32, (count, count * groups), 0)
        col = lax.broadcasted_iota(jnp.int32, (count, count * groups), 1)
        chosen = jnp.where(col == row * groups + g, 1.0, 0.0).astype(jnp.bfloat16)
        return jnp.dot(chosen, raw_ref[...], preferred_element_type=jnp.float32).astype(
            jnp.bfloat16
        )

    loads[0].wait()
    loads[1].wait()
    for g in range(groups):
        kv[me, g, :, :width] = pick(key_ref, g)
        kv[me, g, :, width:] = pick(value_ref, g)
    pl.semaphore_wait(barrier, 4)

    def copy(direction, b, g, target):
        return pltpu.make_async_remote_copy(
            src_ref=kv.at[b, g],
            dst_ref=kv.at[b, g],
            send_sem=send_sem.at[direction, b, g],
            recv_sem=recv_sem.at[b, g],
            device_id={"pipe": target},
            device_id_type=MESH,
        )

    def down_if(zb):
        return (zb >= z) & (zb < rows_r) & (z > 0)

    def up_if(zb):
        return (zb >= 0) & (zb <= z) & (z + 1 <= rows_r - 1 - zb)

    def across_if(zb):
        return (zb >= 0) & (zb < rows_r) & (z <= rows_r - 1 - zb)

    def sends(zb, g, act, downward, upward):
        b = zb * 2 + c
        if downward:

            @pl.when(down_if(zb))
            def _():
                act(copy(0, b, g, me - 2))

        if upward:

            @pl.when(up_if(zb))
            def _():
                act(copy(1, b, g, me + 2))

        @pl.when(across_if(zb))
        def _():
            act(copy(2, b, g, z * 2 + 1 - c))

    for g in range(groups):
        sends(z, g, lambda dma: dma.start(), True, True)

    for load in loads[2:]:
        load.wait()

    def query(g):
        return q_ref[:, g * per_group : (g + 1) * per_group, :].reshape(columns, width)

    for g in range(groups):
        turned[g] = jnp.transpose(query(g))

    def scores(keys, g):
        return jnp.dot(keys, turned[g], preferred_element_type=jnp.float32)

    def gather(values, weights):
        return lax.dot_general(
            values,
            weights.astype(jnp.bfloat16),
            (((0,), (0,)), ((), ())),
            preferred_element_type=jnp.float32,
        )

    for g in range(groups):
        s = scores(pick(own_k_ref, g), g)
        key_index = lax.broadcasted_iota(jnp.int32, s.shape, 0)
        row_index = lax.broadcasted_iota(jnp.int32, s.shape, 1) // per_group
        s = jnp.where(key_index <= row_index, s, -1e30)
        m = jnp.max(s, axis=0, keepdims=True)
        w = jnp.exp2((s - m) * scale)
        top[g] = m
        total[g] = jnp.sum(w, axis=0, keepdims=True)
        acc[g] = gather(pick(own_v_ref, g), w)

    prefix = prefix_ref[me]

    def absorb(b, g):
        s = scores(kv[b, g, :, :width], g)
        key_index = lax.broadcasted_iota(jnp.int32, s.shape, 0)
        s = jnp.where(key_index < prefix - b * block, s, -1e30)
        old = top[g]
        m = jnp.maximum(old, jnp.max(s, axis=0, keepdims=True))
        w = jnp.exp2((s - m) * scale)
        fade = jnp.exp2((old - m) * scale)
        top[g] = m
        total[g] = total[g] * fade + jnp.sum(w, axis=0, keepdims=True)
        acc[g] = acc[g] * fade + gather(kv[b, g, :, width:], w)

    def wait_recv(b, g):
        copy(0, b, g, me).wait_recv()

    def from_above(d):
        return (d > 0) & (z + d < rows_r)

    def from_below(d):
        return (d > 0) & (z - d >= 0) & (z <= rows_r - 1 - (z - d))

    def step(d, carry):
        for g in range(groups):

            @pl.when(from_above(d))
            def _():
                wait_recv((z + d) * 2 + c, g)
                sends(z + d, g, lambda dma: dma.start(), True, False)

            @pl.when(from_below(d))
            def _():
                wait_recv((z - d) * 2 + c, g)
                sends(z - d, g, lambda dma: dma.start(), False, True)

        def use(j, inner):
            crossing = j // 2
            sign = 1 - 2 * (j % 2)
            reach = d - crossing
            zb = z + sign * reach
            b = zb * 2 + jnp.where(crossing == 1, 1 - c, c)
            there = (reach >= 0) & (zb >= 0) & (zb < rows_r) & ((reach > 0) | (sign > 0))
            needed = there & (b <= n - 1 - me)

            @pl.when(needed)
            def _():
                @pl.when(crossing == 1)
                def _():
                    for g in range(groups):
                        wait_recv(b, g)

                for g in range(groups):
                    absorb(b, g)

            return inner

        lax.fori_loop(0, 4, use, 0)
        return carry

    lax.fori_loop(0, rows_r, step, 0)

    def leave(g, source, target, sems, target_ref):
        part = pl.ds(g * per_group, per_group)
        return pltpu.make_async_remote_copy(
            src_ref=source.at[:, part, :],
            dst_ref=target_ref.at[:, part, :],
            send_sem=sems[0].at[g],
            recv_sem=sems[1].at[g],
            device_id={"pipe": target},
            device_id_type=MESH,
        )

    def direct(g):
        return leave(g, stage, (me + 1) % n, (out_send, out_recv), out_ref)

    far = rows_r - 1 - z
    far_block = far * 2 + 1 - c
    for g in range(groups):

        @pl.when((z == 0) | (z == rows_r - 1))
        def _():
            wait_recv(far_block, g)
            absorb(far_block, g)

        done = jnp.transpose(acc[g] / total[g])
        part = pl.ds(g * per_group, per_group)
        stage[:, part, :] = done.astype(jnp.bfloat16).reshape(slice_rows, per_group, width)

        direct(g).start()

    def drain(d, carry):
        for g in range(groups):

            @pl.when(from_above(d))
            def _():
                sends(z + d, g, lambda dma: dma.wait_send(), True, False)

            @pl.when(from_below(d))
            def _():
                sends(z - d, g, lambda dma: dma.wait_send(), False, True)

        return carry

    for g in range(groups):
        sends(z, g, lambda dma: dma.wait_send(), True, True)
    lax.fori_loop(1, rows_r, drain, 0)
    for g in range(groups):
        direct(g).wait()


def fused(queries, slice_own_keys, slice_own_values, cache_keys, context_value_rows, prefix_len):
    n = lax.axis_size("pipe")
    slice_rows, heads, width = queries.shape
    block, groups, _ = cache_keys.shape
    columns = slice_rows * heads // groups
    return pl.pallas_call(
        functools.partial(attend_kernel, n),
        out_shape=jax.ShapeDtypeStruct(queries.shape, jnp.bfloat16),
        in_specs=[pl.BlockSpec(memory_space=pltpu.HBM)] * 6,
        out_specs=pl.BlockSpec(memory_space=pltpu.VMEM),
        scratch_shapes=[
            pltpu.SMEM(prefix_len.shape, jnp.int32),
            pltpu.VMEM(queries.shape, jnp.bfloat16),
            pltpu.VMEM((slice_rows * groups, width), jnp.bfloat16),
            pltpu.VMEM((slice_rows * groups, width), jnp.bfloat16),
            pltpu.VMEM((block * groups, width), jnp.bfloat16),
            pltpu.VMEM((block * groups, width), jnp.bfloat16),
            pltpu.SemaphoreType.DMA((6,)),
            pltpu.VMEM((n, groups, block, 2 * width), jnp.bfloat16),
            pltpu.VMEM((groups, width, columns), jnp.bfloat16),
            pltpu.VMEM((groups, width, columns), jnp.float32),
            pltpu.VMEM((groups, 1, columns), jnp.float32),
            pltpu.VMEM((groups, 1, columns), jnp.float32),
            pltpu.VMEM(queries.shape, jnp.bfloat16),
            pltpu.SemaphoreType.DMA((3, n, groups)),
            pltpu.SemaphoreType.DMA((n, groups)),
            pltpu.SemaphoreType.DMA((groups,)),
            pltpu.SemaphoreType.DMA((groups,)),
        ],
        compiler_params=pltpu.CompilerParams(
            collective_id=0, has_side_effects=True, vmem_limit_bytes=63 * 1024 * 1024
        ),
        name="relay_attention",
    )(
        prefix_len,
        queries,
        slice_own_keys.reshape(-1, width),
        slice_own_values.reshape(-1, width),
        cache_keys.reshape(-1, width),
        context_value_rows.reshape(-1, width),
    )


def solution(mesh):
    in_specs = (
        P(("grp", "pipe"), "head", None),
        P(("grp", "pipe"), "head", None),
        P(("grp", "pipe"), "head", None),
        P(("grp", "pipe"), "head", None),
        P(("grp", "pipe"), "head", None),
        P("grp"),
    )
    out_specs = P(("grp", "pipe"), "head", None)
    return jax.shard_map(fused, mesh=mesh, in_specs=in_specs, out_specs=out_specs, check_vma=False)
```
